32 devices in a mesh: heads: 4 (over y, x), seq: 8 (over z, core).
Axes of the slice: x: 2, y: 2, z: 4, core: 2. Of those that a mesh axis runs over, the one named last changes fastest.
Arguments:
- queries: bfloat16 [4096, 2048], P('seq', 'heads'), may hold values from -64 to 64
- keys: bfloat16 [4096, 512], P('seq', 'heads'), may hold values from -6 to 6
- values: bfloat16 [4096, 512], P('seq', 'heads'), may hold values from -6 to 6
- vertical: int32 [16, 16], replicated, may hold values from 0 to 63, as said below
- slash: int32 [16, 8], replicated, may hold values from 0 to 15, as said below
- out_weight: bfloat16 [2048, 4096], P('heads'), may hold values from -0.25 to 0.25
Outputs:
- layer_out: bfloat16 [4096, 4096], P('seq', 'heads')
The draws below stay inside these ranges and needn't reach their ends.
Inputs may be any that keep to these rules, and one draw needn't show every extreme that they name: `vertical`: each row lists 16 distinct blocks; the four rows of one KV head (rows 4g to 4g+3) list 64 distinct blocks in all; at most 8 of those lie within blocks k * 8 to (k + 1) * 8 - 1 for any k, and in every draw some k reaches 8. `slash`: each row lists 8 distinct offsets, 0 among them; some row holds 15 in every draw.
All inputs are finite; a program needn't handle non-finite values.
Results may differ from the reference program's by a relative error of at most 0.0095.
Values may be sent and summed in bfloat16 or wider, within the bound.
A program may use at most 128 MiB of HBM per device.

```python
import math
import jax
import jax.numpy as jnp
from jax import lax

D = 4096
HEAD_SIZE = 128
BLOCK_TOKENS = 64
VERTICAL_COUNT = 16
NS = 8
KEY_VALUE_HEADS = 4
QUERY_HEADS = 16
BLK_DEV = 8
SEQUENCE_TOKENS = 4096
NB = 64
U = 64
MV = 8


def joint_draw(key):
    base = jax.random.fold_in(key, 11)
    random_key_first, key_b = jax.random.split(base, 2)
    key_entries = jnp.clip(jax.random.normal(random_key_first, (SEQUENCE_TOKENS, KEY_VALUE_HEADS * HEAD_SIZE)), -6.0, 6.0)
    query_vals = 1.5 * jnp.clip(jax.random.normal(key_b, (SEQUENCE_TOKENS, QUERY_HEADS * HEAD_SIZE)), -6.0, 6.0)
    return (query_vals, key_entries)


def draw_queries(key, part):
    query_vals, key_entries = joint_draw(key)
    return query_vals.astype(jnp.float32).astype(jnp.bfloat16)


def draw_keys(key, part):
    query_vals, key_entries = joint_draw(key)
    return key_entries.astype(jnp.float32).astype(jnp.bfloat16)


def draw_vertical(key, part):
    ranges = NB // BLK_DEV
    span = BLK_DEV // MV
    output_rows = []
    for index_in_group in range(KEY_VALUE_HEADS):
        group_key = jax.random.fold_in(key, 100 + index_in_group)
        key_one, key_two, random_key_third, key_four = jax.random.split(group_key, 4)
        full_range = jax.random.randint(key_one, (), 0, ranges)
        others = jax.random.permutation(key_two, (ranges - 1) * MV)[:U - MV]
        other_range = others // MV
        other_range = other_range + (other_range >= full_range).astype(jnp.int32)
        other_pos = others % MV
        range_all = jnp.concatenate([jnp.full((MV,), full_range, jnp.int32), other_range.astype(jnp.int32)])
        pos_all = jnp.concatenate([jnp.arange(MV, dtype=jnp.int32), other_pos.astype(jnp.int32)])
        block_list = range_all * BLK_DEV + pos_all * span + jax.random.randint(random_key_third, (U,), 0, span)
        random_order = jax.random.permutation(key_four, U)
        output_rows.append(block_list[random_order].reshape(QUERY_HEADS // KEY_VALUE_HEADS, VERTICAL_COUNT))
    return jnp.concatenate(output_rows, axis=0).astype(jnp.int32)


def draw_slash(key, part):
    far_row = jax.random.randint(jax.random.fold_in(key, 500), (), 0, QUERY_HEADS)
    output_rows = []
    for row_index in range(QUERY_HEADS):
        perm = jax.random.permutation(jax.random.fold_in(key, 600 + row_index), 2 * BLK_DEV - 2) + 1
        last = jnp.where(row_index == far_row, 2 * BLK_DEV - 1, perm[NS - 2])
        row = jnp.concatenate([jnp.zeros((1,), jnp.int32), perm[:NS - 2].astype(jnp.int32), jnp.reshape(last, (1,)).astype(jnp.int32)])
        output_rows.append(row)
    return jnp.stack(output_rows).astype(jnp.int32)


def block_levels(key, shape, cuts, smallest, top_value):
    loudness, own = 1.0, jax.random.fold_in(key, 6)
    for axis_at, blocks in cuts:
        steps = jnp.exp(jax.random.uniform(jax.random.fold_in(own, axis_at), (blocks,), jnp.float32, smallest / len(cuts), top_value / len(cuts)))
        loudness = loudness * jnp.repeat(steps, shape[axis_at] // blocks).reshape([-1 if axis == axis_at else 1 for axis in range(len(shape))])
    return loudness


def noise(stream_key, shape, deviation, reach, cuts=(), kind=jnp.bfloat16):
    factor_of = block_levels(stream_key, shape, cuts, -0.22, 0.18) if cuts else 1.0
    values = jax.random.normal(stream_key, shape, jnp.float32) * deviation * factor_of
    return jnp.minimum(jnp.maximum(values, -reach), reach).astype(kind)


def setup_inputs(seed: int = 0) -> dict:
    arg_keys = jax.random.split(jax.random.key(seed), 7)
    queries = draw_queries(jax.random.fold_in(arg_keys[6], 71), 0)
    keys = draw_keys(jax.random.fold_in(arg_keys[6], 71), 0)
    values = noise(arg_keys[2], (SEQUENCE_TOKENS, KEY_VALUE_HEADS * HEAD_SIZE), 1.0, 6.0, ((0, 8), (1, 4)))
    vertical = draw_vertical(jax.random.fold_in(arg_keys[6], 71), 0)
    slash = draw_slash(jax.random.fold_in(arg_keys[6], 71), 0)
    out_weight = noise(arg_keys[5], (QUERY_HEADS * HEAD_SIZE, D), (4 * HEAD_SIZE) ** -0.5, 0.25, ((0, 4),))
    return dict(queries=queries, keys=keys, values=values, vertical=vertical, slash=slash, out_weight=out_weight)


def reference(queries, keys, values, vertical, slash, out_weight):
    token_count = queries.shape[0]
    total_blocks = token_count // BLOCK_TOKENS
    heads_per_group = QUERY_HEADS // KEY_VALUE_HEADS
    score_scale = 1.0 / math.sqrt(HEAD_SIZE)
    query_all = queries.reshape(total_blocks, BLOCK_TOKENS, QUERY_HEADS, HEAD_SIZE)
    key_head_rows = keys.reshape(total_blocks, BLOCK_TOKENS, KEY_VALUE_HEADS, HEAD_SIZE).transpose(2, 0, 1, 3)
    value_head_rows = values.reshape(total_blocks, BLOCK_TOKENS, KEY_VALUE_HEADS, HEAD_SIZE).transpose(2, 0, 1, 3)
    owner_head = (jnp.arange(QUERY_HEADS) // heads_per_group).astype(jnp.int32)
    token_pos = jnp.arange(BLOCK_TOKENS)
    causal_tri = token_pos[None, :] <= token_pos[:, None]
    vert_keys = key_head_rows[owner_head[:, None], vertical].astype(jnp.float32)
    vert_values = value_head_rows[owner_head[:, None], vertical].astype(jnp.float32)

    def one_block(block_index):
        query_rows = query_all[block_index].astype(jnp.float32)
        target = block_index - slash
        listed = jnp.any(vertical[:, :, None] == target[:, None, :], axis=1)
        keep = (target >= 0) & jnp.logical_not(listed)
        safe_target = jnp.maximum(target, 0).astype(jnp.int32)
        diag_keys = key_head_rows[owner_head[:, None], safe_target].astype(jnp.float32)
        diag_values = value_head_rows[owner_head[:, None], safe_target].astype(jnp.float32)
        score_vert = jnp.einsum('bhd,hnkd->bhnk', query_rows, vert_keys) * score_scale
        score_diag = jnp.einsum('bhd,hnkd->bhnk', query_rows, diag_keys) * score_scale
        allow_vert = (vertical < block_index)[None, :, :, None] | (vertical == block_index)[None, :, :, None] & causal_tri[:, None, None, :]
        allow_diag = keep[None, :, :, None] & ((slash != 0)[None, :, :, None] | causal_tri[:, None, None, :])
        scores = jnp.concatenate([score_vert.reshape(BLOCK_TOKENS, QUERY_HEADS, -1), score_diag.reshape(BLOCK_TOKENS, QUERY_HEADS, -1)], axis=2)
        allowed = jnp.concatenate([allow_vert.reshape(BLOCK_TOKENS, QUERY_HEADS, -1), allow_diag.reshape(BLOCK_TOKENS, QUERY_HEADS, -1)], axis=2)
        row_top = lax.optimization_barrier(jnp.max(jnp.where(allowed, scores, -jnp.inf), axis=2, keepdims=True))
        expo = jnp.where(allowed, jnp.exp(scores - row_top), 0.0)
        row_total = lax.optimization_barrier(jnp.sum(expo, axis=2, keepdims=True))
        weights = (expo / row_total).astype(jnp.bfloat16).astype(jnp.float32)
        split_at = vertical.shape[1] * BLOCK_TOKENS
        weight_vert = weights[:, :, :split_at].reshape(BLOCK_TOKENS, QUERY_HEADS, -1, BLOCK_TOKENS)
        weight_diag = weights[:, :, split_at:].reshape(BLOCK_TOKENS, QUERY_HEADS, -1, BLOCK_TOKENS)
        result = jnp.einsum('bhnk,hnkd->bhd', weight_vert, vert_values) + jnp.einsum('bhnk,hnkd->bhd', weight_diag, diag_values)
        return result.astype(jnp.bfloat16)
    attention = lax.map(one_block, jnp.arange(total_blocks).astype(jnp.int32))
    attention = attention.reshape(token_count, QUERY_HEADS * HEAD_SIZE)
    group_width = heads_per_group * HEAD_SIZE
    summed = jnp.zeros((token_count, out_weight.shape[1]), jnp.float32)
    for index_in_group in range(KEY_VALUE_HEADS):
        lo_col = index_in_group * group_width
        part = jnp.dot(attention[:, lo_col:lo_col + group_width], out_weight[lo_col:lo_col + group_width], preferred_element_type=jnp.float32).astype(jnp.bfloat16)
        summed = summed + lax.optimization_barrier(part).astype(jnp.float32)
    return summed.astype(jnp.bfloat16)
```

```python
import functools
import math

import jax
import jax.numpy as jnp
from jax import lax
from jax.experimental import pallas as pl
from jax.experimental.pallas import tpu as pltpu
from jax.sharding import PartitionSpec as P

HEAD = 128
BLOCK = 64
CHUNK = 128
REACH = 16
BAND = REACH * BLOCK + CHUNK
MASKED = -1e30
MESH = pl.DeviceIdType.MESH


def kernel(
    n_heads, n_seq, vertical, slash, q_hbm, k_hbm, v_hbm, w_hbm, out,
    q, kall, vall, kvert, vvert, wfull, abuf, bias_band, bias_vert,
    local_sem, kv_send, kv_recv, fwd_send, fwd_recv,
    w_send, w_recv, wf_send, wf_recv, a_send, a_recv,
):
    g = lax.axis_index("heads")
    s = lax.axis_index("seq")
    tokens, width = q.shape
    heads = width // HEAD
    cols = out.shape[1]
    listed = vertical.shape[1]
    vert_rows = listed * BLOCK
    n_chips = n_seq // 2
    chip, core = s // 2, s % 2
    sibling = chip * 2 + 1 - core
    first = s * (tokens // BLOCK)
    half = width // 2
    n_chunks = tokens // CHUNK
    blocks = tokens // BLOCK
    per_chunk = CHUNK // BLOCK

    barrier = pltpu.get_barrier_semaphore()
    for k in range(1, n_heads):
        pl.semaphore_signal(barrier, inc=1, device_id={"heads": (g + k) % n_heads}, device_id_type=MESH)
    pl.semaphore_signal(barrier, inc=1, device_id={"seq": sibling}, device_id_type=MESH)

    @pl.loop(1, n_chips)
    def _(d):
        pl.semaphore_signal(
            barrier, inc=1, device_id={"seq": ((chip + d) % n_chips) * 2 + core}, device_id_type=MESH
        )

    def shard(index):
        return pl.ds((index + 2) * blocks, blocks)

    def rows_of_w(group, part):
        return pl.ds(pl.multiple_of(group * width + part * half, half), half)

    own = [
        pltpu.make_async_copy(k_hbm, kall.at[shard(s)], local_sem.at[0]),
        pltpu.make_async_copy(v_hbm, vall.at[shard(s)], local_sem.at[1]),
        pltpu.make_async_copy(q_hbm, q, local_sem.at[2]),
        pltpu.make_async_copy(
            w_hbm.at[:, pl.ds(pl.multiple_of(g * cols, cols), cols)],
            wfull.at[pl.ds(pl.multiple_of(g * width, width), width)],
            local_sem.at[3],
        ),
    ]
    for copy in own:
        copy.start()
    pl.semaphore_wait(barrier, n_heads + n_chips - 1)

    sources = ((k_hbm, kall), (v_hbm, vall))

    def kv_copy(which, d, index, target):
        src, dst = sources[which]
        return pltpu.make_async_remote_copy(
            src_ref=src, dst_ref=dst.at[shard(index)],
            send_sem=kv_send.at[which, d], recv_sem=kv_recv.at[which, d],
            device_id={"seq": target}, device_id_type=MESH,
        )

    def kv_pass(which, d, index):
        dst = sources[which][1]
        return pltpu.make_async_remote_copy(
            src_ref=dst.at[shard(index)], dst_ref=dst.at[shard(index)],
            send_sem=fwd_send.at[which, d], recv_sem=fwd_recv.at[which, d],
            device_id={"seq": sibling}, device_id_type=MESH,
        )

    def w_copy(k):
        peer = (g + k) % n_heads
        return pltpu.make_async_remote_copy(
            src_ref=w_hbm.at[
                pl.ds(pl.multiple_of(core * half, half), half), pl.ds(pl.multiple_of(peer * cols, cols), cols)
            ],
            dst_ref=wfull.at[rows_of_w(g, core)],
            send_sem=w_send.at[k], recv_sem=w_recv.at[k],
            device_id={"heads": peer}, device_id_type=MESH,
        )

    def w_arrival(k):
        rows = wfull.at[rows_of_w((g + n_heads - k) % n_heads, core)]
        return pltpu.make_async_copy(rows, rows, w_recv.at[k])

    def w_pass(k, part):
        rows = wfull.at[rows_of_w((g + n_heads - k) % n_heads, part)]
        return pltpu.make_async_remote_copy(
            src_ref=rows, dst_ref=rows, send_sem=wf_send.at[k], recv_sem=wf_recv.at[k],
            device_id={"seq": sibling}, device_id_type=MESH,
        )

    @pl.loop(1, n_chips)
    def _(d):
        @pl.when(chip + d < n_chips)
        def _():
            for which in range(2):
                kv_copy(which, d, s, s + 2 * d).start()

    for k in range(1, n_heads):
        w_copy(k).start()

    empty = jnp.zeros((2 * blocks, BLOCK, HEAD), jnp.bfloat16)
    kall[pl.ds(0, 2 * blocks)] = empty
    vall[pl.ds(0, 2 * blocks)] = empty

    @pl.loop(chip + 1, n_chips)
    def _(later):
        at = pl.ds((2 * later + 2) * blocks, 2 * blocks)
        kall[at] = empty
        vall[at] = empty

    row = lax.broadcasted_iota(jnp.int32, (blocks, BAND), 0)
    place = lax.broadcasted_iota(jnp.int32, (blocks, BAND), 1) // BLOCK
    target = first + (row // per_chunk) * per_chunk - REACH + place
    offset = first + row - target
    vrow = lax.broadcasted_iota(jnp.int32, (blocks, vert_rows), 0)
    vplace = lax.broadcasted_iota(jnp.int32, (blocks, vert_rows), 1) // BLOCK

    @pl.loop(0, heads)
    def _(h):
        head = g * heads + h
        hit = jnp.zeros((blocks, BAND), jnp.int32)
        listed_block = jnp.zeros((blocks, vert_rows), jnp.int32)
        for n in range(listed):
            hit = jnp.where(target == vertical[head, n], 1, hit)
            listed_block = jnp.where(vplace == n, vertical[head, n], listed_block)
        for n in range(slash.shape[1]):
            hit = jnp.where(offset == slash[head, n], 1, hit)
        seen = (hit == 1) & (offset >= 0) & (offset < REACH) & (target >= 0)
        at = pl.ds(pl.multiple_of(h * blocks, blocks), blocks)
        bias_band[at, :] = jnp.where(seen, 0.0, MASKED)
        bias_vert[at, :] = jnp.where(listed_block <= first + vrow - REACH, 0.0, MASKED)

    own[0].wait()
    own[1].wait()
    for which in range(2):
        kv_pass(which, 0, s).start()

    @pl.loop(1, n_chips)
    def _(d):
        @pl.when(chip >= d)
        def _():
            for which in range(2):
                kv_copy(which, d, s - 2 * d, s).wait_recv()
                kv_pass(which, d, s - 2 * d).start()

    @pl.loop(0, n_chips)
    def _(d):
        @pl.when(chip >= d)
        def _():
            for which in range(2):
                kv_pass(which, d, sibling - 2 * d).wait_recv()

    own[2].wait()

    @pl.loop(0, heads * listed)
    def _(i):
        block = vertical[g * heads + i // listed, i % listed] + 2 * blocks
        kvert[i] = kall[block]
        vvert[i] = vall[block]

    scale = math.log2(math.e) / math.sqrt(HEAD)
    across = (((1,), (1,)), ((), ()))
    wide = REACH * BLOCK

    def chunk_rows(c):
        return pl.ds(pl.multiple_of(c * CHUNK, CHUNK), CHUNK)

    def group_cols(group):
        return pl.ds(pl.multiple_of(group * width, width), width)

    def a_copy(c, k):
        part = abuf.at[chunk_rows(c), group_cols(g)]
        return pltpu.make_async_remote_copy(
            src_ref=part, dst_ref=part, send_sem=a_send.at[c, k], recv_sem=a_recv.at[c, k],
            device_id={"heads": (g + k) % n_heads}, device_id_type=MESH,
        )

    def a_arrival(c, k):
        part = abuf.at[chunk_rows(c), group_cols((g + n_heads - k) % n_heads)]
        return pltpu.make_async_copy(part, part, a_recv.at[c, k])

    def spread(ref, h, c):
        rows = [
            jnp.broadcast_to(ref[pl.ds(h * blocks + c * per_chunk + a, 1), :], (BLOCK, ref.shape[1]))
            for a in range(per_chunk)
        ]
        return jnp.concatenate(rows, axis=0)

    @pl.loop(0, n_chunks)
    def _(c):
        base = first + c * per_chunk

        @pl.loop(0, heads)
        def _(h):
            col = pl.multiple_of(h * HEAD, HEAD)
            qh = q[chunk_rows(c), pl.ds(col, HEAD)]
            vrows = pl.ds(h * listed, listed)

            def flat(ref, at):
                return ref[at].reshape(at.size * BLOCK, HEAD)

            band = lax.dot_general(qh, flat(kall, pl.ds(base, REACH + per_chunk)), across, preferred_element_type=jnp.float32)
            vert = lax.dot_general(qh, flat(kvert, vrows), across, preferred_element_type=jnp.float32)
            band = band * scale + spread(bias_band, h, c)
            vert = vert * scale + spread(bias_vert, h, c)
            i = lax.broadcasted_iota(jnp.int32, (CHUNK, CHUNK), 0)
            j = lax.broadcasted_iota(jnp.int32, (CHUNK, CHUNK), 1)
            near = jnp.where(j <= i, band[:, wide:], MASKED)
            band = band[:, :wide]
            top = jnp.maximum(
                jnp.maximum(jnp.max(band, axis=1, keepdims=True), jnp.max(vert, axis=1, keepdims=True)),
                jnp.max(near, axis=1, keepdims=True),
            )
            band, vert, near = jnp.exp2(band - top), jnp.exp2(vert - top), jnp.exp2(near - top)
            total = (
                jnp.sum(band, axis=1, keepdims=True)
                + jnp.sum(vert, axis=1, keepdims=True)
                + jnp.sum(near, axis=1, keepdims=True)
            )
            mixed = jnp.dot(band.astype(jnp.bfloat16), flat(vall, pl.ds(base, REACH)), preferred_element_type=jnp.float32)
            mixed += jnp.dot(near.astype(jnp.bfloat16), flat(vall, pl.ds(base + REACH, per_chunk)), preferred_element_type=jnp.float32)
            mixed += jnp.dot(vert.astype(jnp.bfloat16), flat(vvert, vrows), preferred_element_type=jnp.float32)
            abuf[chunk_rows(c), pl.ds(pl.multiple_of(g * width + h * HEAD, HEAD), HEAD)] = (
                mixed / total
            ).astype(jnp.bfloat16)

        for k in range(1, n_heads):
            a_copy(c, k).start()

    own[3].wait()
    for k in range(1, n_heads):
        w_arrival(k).wait()
        w_pass(k, core).start()
    for k in range(1, n_heads):
        w_pass(k, 1 - core).wait_recv()

    tile = min(cols, 256)

    @pl.loop(0, n_chunks)
    def _(c):
        for k in range(1, n_heads):
            a_arrival(c, k).wait()

        @pl.loop(0, cols // tile)
        def _(t):
            at = pl.ds(pl.multiple_of(t * tile, tile), tile)
            out[chunk_rows(c), at] = jnp.dot(
                abuf[chunk_rows(c), :], wfull[:, at], preferred_element_type=jnp.float32
            ).astype(out.dtype)

    @pl.loop(0, n_chunks)
    def _(c):
        for k in range(1, n_heads):
            a_copy(c, k).wait_send()

    for k in range(1, n_heads):
        w_copy(k).wait_send()
        w_pass(k, core).wait_send()

    for which in range(2):
        kv_pass(which, 0, s).wait_send()

    @pl.loop(1, n_chips)
    def _(d):
        @pl.when(chip + d < n_chips)
        def _():
            for which in range(2):
                kv_copy(which, d, s, s + 2 * d).wait_send()

        @pl.when(chip >= d)
        def _():
            for which in range(2):
                kv_pass(which, d, s - 2 * d).wait_send()


def local(n_heads, n_seq, queries, keys, values, vertical, slash, out_weight):
    tokens, width = queries.shape
    cols = out_weight.shape[1] // n_heads
    heads = width // HEAD
    blocks = tokens // BLOCK
    n_chips = n_seq // 2
    n_chunks = tokens // CHUNK
    vert_rows = vertical.shape[1] * BLOCK
    bf16, dma = jnp.bfloat16, pltpu.SemaphoreType.DMA
    smem = pl.BlockSpec(memory_space=pltpu.SMEM)
    hbm = pl.BlockSpec(memory_space=pltpu.HBM)
    scores = heads * tokens * (BAND + vert_rows)
    return pl.pallas_call(
        functools.partial(kernel, n_heads, n_seq),
        out_shape=jax.ShapeDtypeStruct((tokens, cols), bf16),
        in_specs=[smem, smem, hbm, hbm, hbm, hbm],
        out_specs=pl.BlockSpec(memory_space=pltpu.VMEM),
        scratch_shapes=[
            pltpu.VMEM((tokens, width), bf16),
            pltpu.VMEM(((n_seq + 2) * blocks, BLOCK, HEAD), bf16),
            pltpu.VMEM(((n_seq + 2) * blocks, BLOCK, HEAD), bf16),
            pltpu.VMEM((heads * vertical.shape[1], BLOCK, HEAD), bf16),
            pltpu.VMEM((heads * vertical.shape[1], BLOCK, HEAD), bf16),
            pltpu.VMEM((n_heads * width, cols), bf16),
            pltpu.VMEM((tokens, n_heads * width), bf16),
            pltpu.VMEM((heads * blocks, BAND), jnp.float32),
            pltpu.VMEM((heads * blocks, vert_rows), jnp.float32),
            dma((4,)),
            dma((2, n_chips)), dma((2, n_chips)), dma((2, n_chips)), dma((2, n_chips)),
            dma((n_heads,)), dma((n_heads,)), dma((n_heads,)), dma((n_heads,)),
            dma((n_chunks, n_heads)), dma((n_chunks, n_heads)),
        ],
        compiler_params=pltpu.CompilerParams(
            collective_id=0, has_side_effects=True, vmem_limit_bytes=48 * 1024 * 1024
        ),
        cost_estimate=pl.CostEstimate(
            flops=4 * scores * HEAD + 2 * tokens * n_heads * width * cols,
            bytes_accessed=8 * 1024 * 1024,
            transcendentals=scores,
        ),
    )(
        vertical, slash, queries,
        keys.reshape(blocks, BLOCK, HEAD), values.reshape(blocks, BLOCK, HEAD), out_weight,
    )


def solution(mesh):
    sizes = dict(mesh.shape)
    return jax.shard_map(
        functools.partial(local, sizes["heads"], sizes["seq"]),
        mesh=mesh,
        in_specs=(P("seq", "heads"), P("seq", "heads"), P("seq", "heads"), P(), P(), P("heads", None)),
        out_specs=P("seq", "heads"),
        check_vma=False,
    )
```

```python
import functools
import math

import jax
import jax.numpy as jnp
from jax import lax
from jax.experimental import pallas as pl
from jax.experimental.pallas import tpu as pltpu
from jax.sharding import PartitionSpec as P

HEAD = 128
BLOCK = 64
CHUNK = 128
REACH = 16
BAND = REACH * BLOCK + CHUNK
MASKED = -1e30
MESH = pl.DeviceIdType.MESH


def kernel(
    n_heads, n_seq, vertical, slash, q_hbm, k_hbm, v_hbm, w_hbm, out,
    q, kall, vall, kvert, vvert, wfull, abuf, bias_band, bias_vert,
    local_sem, kv_send, kv_recv, fwd_send, fwd_recv,
    w_send, w_recv, wf_send, wf_recv, a_send, a_recv, r_send, r_recv,
):
    g = lax.axis_index("heads")
    s = lax.axis_index("seq")
    tokens, width = q.shape
    heads = width // HEAD
    cols = out.shape[1]
    listed = vertical.shape[1]
    vert_rows = listed * BLOCK
    n_chips = n_seq // 2
    chip, core = s // 2, s % 2
    sibling = chip * 2 + 1 - core
    first = s * (tokens // BLOCK)
    half = width // 2
    n_chunks = tokens // CHUNK
    blocks = tokens // BLOCK
    per_chunk = CHUNK // BLOCK

    barrier = pltpu.get_barrier_semaphore()
    for k in range(1, n_heads):
        pl.semaphore_signal(barrier, inc=1, device_id={"heads": (g + k) % n_heads}, device_id_type=MESH)
    pl.semaphore_signal(barrier, inc=1, device_id={"seq": sibling}, device_id_type=MESH)

    above, below = chip + 1 < n_chips, chip > 0

    @pl.when(above)
    def _():
        pl.semaphore_signal(barrier, inc=1, device_id={"seq": s + 2}, device_id_type=MESH)

    @pl.when(below)
    def _():
        pl.semaphore_signal(barrier, inc=1, device_id={"seq": s - 2}, device_id_type=MESH)

    def shard(index):
        return pl.ds((index + 2) * blocks, blocks)

    def rows_of_w(group, part):
        return pl.ds(pl.multiple_of(group * width + part * half, half), half)

    own = [
        pltpu.make_async_copy(k_hbm, kall.at[shard(s)], local_sem.at[0]),
        pltpu.make_async_copy(v_hbm, vall.at[shard(s)], local_sem.at[1]),
        pltpu.make_async_copy(q_hbm, q, local_sem.at[2]),
        pltpu.make_async_copy(
            w_hbm.at[:, pl.ds(pl.multiple_of(g * cols, cols), cols)],
            wfull.at[pl.ds(pl.multiple_of(g * width, width), width)],
            local_sem.at[3],
        ),
    ]
    for copy in own:
        copy.start()
    neighbours = (chip + n_chips - 1) // n_chips + (2 * n_chips - 2 - chip) // n_chips
    pl.semaphore_wait(barrier, n_heads + neighbours)

    sources = ((k_hbm, kall), (v_hbm, vall))

    def kv_first(which):
        src, dst = sources[which]
        return pltpu.make_async_remote_copy(
            src_ref=src, dst_ref=dst.at[shard(s)],
            send_sem=kv_send.at[which, 0], recv_sem=kv_recv.at[which, 0],
            device_id={"seq": s + 2}, device_id_type=MESH,
        )

    def kv_copy(which, d, index):
        dst = sources[which][1]
        return pltpu.make_async_remote_copy(
            src_ref=dst.at[shard(index)], dst_ref=dst.at[shard(index)],
            send_sem=kv_send.at[which, d], recv_sem=kv_recv.at[which, d],
            device_id={"seq": s + 2}, device_id_type=MESH,
        )

    def kv_pass(which, d, index):
        dst = sources[which][1]
        return pltpu.make_async_remote_copy(
            src_ref=dst.at[shard(index)], dst_ref=dst.at[shard(index)],
            send_sem=fwd_send.at[which, d], recv_sem=fwd_recv.at[which, d],
            device_id={"seq": sibling}, device_id_type=MESH,
        )

    def w_copy(k):
        peer = (g + k) % n_heads
        return pltpu.make_async_remote_copy(
            src_ref=w_hbm.at[
                pl.ds(pl.multiple_of(core * half, half), half), pl.ds(pl.multiple_of(peer * cols, cols), cols)
            ],
            dst_ref=wfull.at[rows_of_w(g, core)],
            send_sem=w_send.at[k], recv_sem=w_recv.at[k],
            device_id={"heads": peer}, device_id_type=MESH,
        )

    def w_arrival(k):
        rows = wfull.at[rows_of_w((g + n_heads - k) % n_heads, core)]
        return pltpu.make_async_copy(rows, rows, w_recv.at[k])

    def w_pass(k, part):
        rows = wfull.at[rows_of_w((g + n_heads - k) % n_heads, part)]
        return pltpu.make_async_remote_copy(
            src_ref=rows, dst_ref=rows, send_sem=wf_send.at[k], recv_sem=wf_recv.at[k],
            device_id={"seq": sibling}, device_id_type=MESH,
        )

    @pl.when(above)
    def _():
        for which in range(2):
            kv_first(which).start()

    for k in range(1, n_heads):
        w_copy(k).start()

    empty = jnp.zeros((2 * blocks, BLOCK, HEAD), jnp.bfloat16)
    kall[pl.ds(0, 2 * blocks)] = empty
    vall[pl.ds(0, 2 * blocks)] = empty

    @pl.loop(chip + 1, n_chips)
    def _(later):
        at = pl.ds((2 * later + 2) * blocks, 2 * blocks)
        kall[at] = empty
        vall[at] = empty

    row = lax.broadcasted_iota(jnp.int32, (blocks, BAND), 0)
    place = lax.broadcasted_iota(jnp.int32, (blocks, BAND), 1) // BLOCK
    target = first + (row // per_chunk) * per_chunk - REACH + place
    offset = first + row - target
    vrow = lax.broadcasted_iota(jnp.int32, (blocks, vert_rows), 0)
    vplace = lax.broadcasted_iota(jnp.int32, (blocks, vert_rows), 1) // BLOCK

    @pl.loop(0, heads)
    def _(h):
        head = g * heads + h
        hit = jnp.zeros((blocks, BAND), jnp.int32)
        listed_block = jnp.zeros((blocks, vert_rows), jnp.int32)
        for n in range(listed):
            hit = jnp.where(target == vertical[head, n], 1, hit)
            listed_block = jnp.where(vplace == n, vertical[head, n], listed_block)
        for n in range(slash.shape[0]):
            hit = jnp.where(offset == slash[n, head], 1, hit)
        seen = (hit == 1) & (offset >= 0) & (offset < REACH) & (target >= 0)
        at = pl.ds(pl.multiple_of(h * blocks, blocks), blocks)
        bias_band[at, :] = jnp.where(seen, 0.0, MASKED)
        bias_vert[at, :] = jnp.where(listed_block <= first + vrow - REACH, 0.0, MASKED)

    own[0].wait()
    own[1].wait()
    for which in range(2):
        kv_pass(which, 0, s).start()

    @pl.loop(1, n_chips)
    def _(d):
        @pl.when(chip >= d)
        def _():
            for which in range(2):
                kv_copy(which, d - 1, s - 2 * d).wait_recv()

                @pl.when(above)
                def _():
                    kv_copy(which, d, s - 2 * d).start()

                kv_pass(which, d, s - 2 * d).start()

    @pl.loop(0, n_chips)
    def _(d):
        @pl.when(chip >= d)
        def _():
            for which in range(2):
                kv_pass(which, d, sibling - 2 * d).wait_recv()

    own[2].wait()

    @pl.loop(0, heads * listed)
    def _(i):
        block = vertical[g * heads + i // listed, i % listed] + 2 * blocks
        kvert[i] = kall[block]
        vvert[i] = vall[block]

    scale = math.log2(math.e) / math.sqrt(HEAD)
    across = (((1,), (1,)), ((), ()))
    wide = REACH * BLOCK

    def chunk_rows(c):
        return pl.ds(pl.multiple_of(c * CHUNK, CHUNK), CHUNK)

    def group_cols(group):
        return pl.ds(pl.multiple_of(group * width, width), width)

    near_groups = (g + 1 - 2 * (g % 2), (g + 2) % 4)
    far = (near_groups[0] + 2) % 4

    def a_copy(c, k):
        part = abuf.at[chunk_rows(c), group_cols(g)]
        return pltpu.make_async_remote_copy(
            src_ref=part, dst_ref=part, send_sem=a_send.at[c, k], recv_sem=a_recv.at[c, k],
            device_id={"heads": near_groups[k]}, device_id_type=MESH,
        )

    def a_arrival(c, k):
        part = abuf.at[chunk_rows(c), group_cols(near_groups[k])]
        return pltpu.make_async_copy(part, part, a_recv.at[c, k])

    def half_rows(c, k):
        return pl.ds(pl.multiple_of(c * CHUNK + k * BLOCK, BLOCK), BLOCK)

    def a_relay(c, k):
        part = abuf.at[half_rows(c, k), group_cols(near_groups[k])]
        return pltpu.make_async_remote_copy(
            src_ref=part, dst_ref=part, send_sem=r_send.at[c, k], recv_sem=r_recv.at[c, k],
            device_id={"heads": near_groups[1 - k]}, device_id_type=MESH,
        )

    def far_arrival(c, k):
        part = abuf.at[half_rows(c, k), group_cols(far)]
        return pltpu.make_async_copy(part, part, r_recv.at[c, k])

    def spread(ref, h, c):
        rows = [
            jnp.broadcast_to(ref[pl.ds(h * blocks + c * per_chunk + a, 1), :], (BLOCK, ref.shape[1]))
            for a in range(per_chunk)
        ]
        return jnp.concatenate(rows, axis=0)

    @pl.loop(0, n_chunks)
    def _(c):
        base = first + c * per_chunk

        @pl.loop(0, heads)
        def _(h):
            col = pl.multiple_of(h * HEAD, HEAD)
            qh = q[chunk_rows(c), pl.ds(col, HEAD)]
            vrows = pl.ds(h * listed, listed)

            def flat(ref, at):
                return ref[at].reshape(at.size * BLOCK, HEAD)

            band = lax.dot_general(qh, flat(kall, pl.ds(base, REACH + per_chunk)), across, preferred_element_type=jnp.float32)
            vert = lax.dot_general(qh, flat(kvert, vrows), across, preferred_element_type=jnp.float32)
            band = band * scale + spread(bias_band, h, c)
            vert = vert * scale + spread(bias_vert, h, c)
            i = lax.broadcasted_iota(jnp.int32, (CHUNK, CHUNK), 0)
            j = lax.broadcasted_iota(jnp.int32, (CHUNK, CHUNK), 1)
            near = jnp.where(j <= i, band[:, wide:], MASKED)
            band = band[:, :wide]
            top = jnp.maximum(
                jnp.maximum(jnp.max(band, axis=1, keepdims=True), jnp.max(vert, axis=1, keepdims=True)),
                jnp.max(near, axis=1, keepdims=True),
            )
            band, vert, near = jnp.exp2(band - top), jnp.exp2(vert - top), jnp.exp2(near - top)
            total = (
                jnp.sum(band, axis=1, keepdims=True)
                + jnp.sum(vert, axis=1, keepdims=True)
                + jnp.sum(near, axis=1, keepdims=True)
            )
            mixed = jnp.dot(band.astype(jnp.bfloat16), flat(vall, pl.ds(base, REACH)), preferred_element_type=jnp.float32)
            mixed += jnp.dot(near.astype(jnp.bfloat16), flat(vall, pl.ds(base + REACH, per_chunk)), preferred_element_type=jnp.float32)
            mixed += jnp.dot(vert.astype(jnp.bfloat16), flat(vvert, vrows), preferred_element_type=jnp.float32)
            abuf[chunk_rows(c), pl.ds(pl.multiple_of(g * width + h * HEAD, HEAD), HEAD)] = (
                mixed / total
            ).astype(jnp.bfloat16)

        for k in range(2):
            a_copy(c, k).start()

    own[3].wait()
    for k in range(1, n_heads):
        w_arrival(k).wait()
        w_pass(k, core).start()
    for k in range(1, n_heads):
        w_pass(k, 1 - core).wait_recv()

    tile = min(cols, 256)

    def project(c):
        for k in range(2):
            far_arrival(c, k).wait()

        @pl.loop(0, cols // tile)
        def _(t):
            at = pl.ds(pl.multiple_of(t * tile, tile), tile)
            out[chunk_rows(c), at] = jnp.dot(
                abuf[chunk_rows(c), :], wfull[:, at], preferred_element_type=jnp.float32
            ).astype(out.dtype)

    @pl.loop(0, n_chunks + 1)
    def _(c):
        @pl.when(c < n_chunks)
        def _():
            for k in range(2):
                a_arrival(c, k).wait()
                a_relay(c, k).start()

        @pl.when(c > 0)
        def _():
            project(c - 1)

    @pl.loop(0, n_chunks)
    def _(c):
        for k in range(2):
            a_copy(c, k).wait_send()
            a_relay(c, k).wait_send()

    for k in range(1, n_heads):
        w_copy(k).wait_send()
        w_pass(k, core).wait_send()

    for which in range(2):
        kv_pass(which, 0, s).wait_send()

    @pl.when(above)
    def _():
        for which in range(2):
            kv_first(which).wait_send()

    @pl.loop(1, n_chips)
    def _(d):
        @pl.when(chip >= d)
        def _():
            for which in range(2):
                kv_pass(which, d, s - 2 * d).wait_send()

                @pl.when(above)
                def _():
                    kv_copy(which, d, s - 2 * d).wait_send()


def local(n_heads, n_seq, queries, keys, values, vertical, slash, out_weight):
    tokens, width = queries.shape
    cols = out_weight.shape[1] // n_heads
    heads = width // HEAD
    blocks = tokens // BLOCK
    n_chips = n_seq // 2
    n_chunks = tokens // CHUNK
    vert_rows = vertical.shape[1] * BLOCK
    bf16, dma = jnp.bfloat16, pltpu.SemaphoreType.DMA
    smem = pl.BlockSpec(memory_space=pltpu.SMEM)
    hbm = pl.BlockSpec(memory_space=pltpu.HBM)
    scores = heads * tokens * (BAND + vert_rows)
    return pl.pallas_call(
        functools.partial(kernel, n_heads, n_seq),
        out_shape=jax.ShapeDtypeStruct((tokens, cols), bf16),
        in_specs=[smem, smem, hbm, hbm, hbm, hbm],
        out_specs=pl.BlockSpec(memory_space=pltpu.VMEM),
        scratch_shapes=[
            pltpu.VMEM((tokens, width), bf16),
            pltpu.VMEM(((n_seq + 2) * blocks, BLOCK, HEAD), bf16),
            pltpu.VMEM(((n_seq + 2) * blocks, BLOCK, HEAD), bf16),
            pltpu.VMEM((heads * vertical.shape[1], BLOCK, HEAD), bf16),
            pltpu.VMEM((heads * vertical.shape[1], BLOCK, HEAD), bf16),
            pltpu.VMEM((n_heads * width, cols), bf16),
            pltpu.VMEM((tokens, n_heads * width), bf16),
            pltpu.VMEM((heads * blocks, BAND), jnp.float32),
            pltpu.VMEM((heads * blocks, vert_rows), jnp.float32),
            dma((4,)),
            dma((2, n_chips)), dma((2, n_chips)), dma((2, n_chips)), dma((2, n_chips)),
            dma((n_heads,)), dma((n_heads,)), dma((n_heads,)), dma((n_heads,)),
            dma((n_chunks, 2)), dma((n_chunks, 2)), dma((n_chunks, 2)), dma((n_chunks, 2)),
        ],
        compiler_params=pltpu.CompilerParams(
            collective_id=0, has_side_effects=True, vmem_limit_bytes=60 * 1024 * 1024
        ),
        cost_estimate=pl.CostEstimate(
            flops=4 * scores * HEAD + 2 * tokens * n_heads * width * cols,
            bytes_accessed=8 * 1024 * 1024,
            transcendentals=scores,
        ),
    )(
        vertical, slash.T, queries,
        keys.reshape(blocks, BLOCK, HEAD), values.reshape(blocks, BLOCK, HEAD), out_weight,
    )


def solution(mesh):
    sizes = dict(mesh.shape)
    return jax.shard_map(
        functools.partial(local, sizes["heads"], sizes["seq"]),
        mesh=mesh,
        in_specs=(P("seq", "heads"), P("seq", "heads"), P("seq", "heads"), P(), P(), P("heads", None)),
        out_specs=P("seq", "heads"),
        check_vma=False,
    )
```

```python
import functools
import math

import jax
import jax.numpy as jnp
from jax import lax
from jax.experimental import pallas as pl
from jax.experimental.pallas import tpu as pltpu
from jax.sharding import PartitionSpec as P

HEAD = 128
BLOCK = 64
CHUNK = 128
REACH = 16
BAND = REACH * BLOCK + CHUNK
MASKED = -1e30
MESH = pl.DeviceIdType.MESH


def kernel(
    n_heads, n_seq, vertical, slash, q_hbm, k_hbm, v_hbm, w_hbm, out,
    q, kall, vall, kvert, vvert, wfull, abuf, bias_band, bias_vert,
    local_sem, kv_send, kv_recv, fwd_send, fwd_recv,
    w_send, w_recv, wf_send, wf_recv, a_send, a_recv, r_send, r_recv,
):
    g = lax.axis_index("heads")
    s = lax.axis_index("seq")
    tokens, width = q.shape
    heads = width // HEAD
    cols = out.shape[1]
    listed = vertical.shape[1]
    vert_rows = listed * BLOCK
    n_chips = n_seq // 2
    chip, core = s // 2, s % 2
    sibling = chip * 2 + 1 - core
    first = s * (tokens // BLOCK)
    half = width // 2
    n_chunks = tokens // CHUNK
    blocks = tokens // BLOCK
    per_chunk = CHUNK // BLOCK

    barrier = pltpu.get_barrier_semaphore()
    for k in range(1, n_heads):
        pl.semaphore_signal(barrier, inc=1, device_id={"heads": (g + k) % n_heads}, device_id_type=MESH)
    pl.semaphore_signal(barrier, inc=1, device_id={"seq": sibling}, device_id_type=MESH)

    above, below = chip + 1 < n_chips, chip > 0

    @pl.when(above)
    def _():
        pl.semaphore_signal(barrier, inc=1, device_id={"seq": s + 2}, device_id_type=MESH)

    @pl.when(below)
    def _():
        pl.semaphore_signal(barrier, inc=1, device_id={"seq": s - 2}, device_id_type=MESH)

    def shard(index):
        return pl.ds((index + 2) * blocks, blocks)

    def rows_of_w(group, part):
        return pl.ds(pl.multiple_of(group * width + part * half, half), half)

    own = [
        pltpu.make_async_copy(k_hbm, kall.at[shard(s)], local_sem.at[0]),
        pltpu.make_async_copy(v_hbm, vall.at[shard(s)], local_sem.at[1]),
        pltpu.make_async_copy(q_hbm, q, local_sem.at[2]),
        pltpu.make_async_copy(
            w_hbm.at[:, pl.ds(pl.multiple_of(g * cols, cols), cols)],
            wfull.at[pl.ds(pl.multiple_of(g * width, width), width)],
            local_sem.at[3],
        ),
    ]
    for copy in own:
        copy.start()
    neighbours = (chip + n_chips - 1) // n_chips + (2 * n_chips - 2 - chip) // n_chips
    pl.semaphore_wait(barrier, n_heads + neighbours)

    sources = ((k_hbm, kall), (v_hbm, vall))

    def kv_first(which):
        src, dst = sources[which]
        return pltpu.make_async_remote_copy(
            src_ref=src, dst_ref=dst.at[shard(s)],
            send_sem=kv_send.at[which, 0], recv_sem=kv_recv.at[which, 0],
            device_id={"seq": s + 2}, device_id_type=MESH,
        )

    def kv_copy(which, d, index):
        dst = sources[which][1]
        return pltpu.make_async_remote_copy(
            src_ref=dst.at[shard(index)], dst_ref=dst.at[shard(index)],
            send_sem=kv_send.at[which, d], recv_sem=kv_recv.at[which, d],
            device_id={"seq": s + 2}, device_id_type=MESH,
        )

    def kv_pass(which, d, index):
        dst = sources[which][1]
        return pltpu.make_async_remote_copy(
            src_ref=dst.at[shard(index)], dst_ref=dst.at[shard(index)],
            send_sem=fwd_send.at[which, d], recv_sem=fwd_recv.at[which, d],
            device_id={"seq": sibling}, device_id_type=MESH,
        )

    def w_copy(k):
        peer = (g + k) % n_heads
        return pltpu.make_async_remote_copy(
            src_ref=w_hbm.at[
                pl.ds(pl.multiple_of(core * half, half), half), pl.ds(pl.multiple_of(peer * cols, cols), cols)
            ],
            dst_ref=wfull.at[rows_of_w(g, core)],
            send_sem=w_send.at[k], recv_sem=w_recv.at[k],
            device_id={"heads": peer}, device_id_type=MESH,
        )

    def w_arrival(k):
        rows = wfull.at[rows_of_w((g + n_heads - k) % n_heads, core)]
        return pltpu.make_async_copy(rows, rows, w_recv.at[k])

    def w_pass(k, part):
        rows = wfull.at[rows_of_w((g + n_heads - k) % n_heads, part)]
        return pltpu.make_async_remote_copy(
            src_ref=rows, dst_ref=rows, send_sem=wf_send.at[k], recv_sem=wf_recv.at[k],
            device_id={"seq": sibling}, device_id_type=MESH,
        )

    @pl.when(above)
    def _():
        for which in range(2):
            kv_first(which).start()

    for k in range(1, n_heads):
        w_copy(k).start()

    empty = jnp.zeros((2 * blocks, BLOCK, HEAD), jnp.bfloat16)
    kall[pl.ds(0, 2 * blocks)] = empty
    vall[pl.ds(0, 2 * blocks)] = empty

    @pl.loop(chip + 1, n_chips)
    def _(later):
        at = pl.ds((2 * later + 2) * blocks, 2 * blocks)
        kall[at] = empty
        vall[at] = empty

    row = lax.broadcasted_iota(jnp.int32, (blocks, BAND), 0)
    place = lax.broadcasted_iota(jnp.int32, (blocks, BAND), 1) // BLOCK
    target = first + (row // per_chunk) * per_chunk - REACH + place
    offset = first + row - target
    vrow = lax.broadcasted_iota(jnp.int32, (blocks, vert_rows), 0)
    vplace = lax.broadcasted_iota(jnp.int32, (blocks, vert_rows), 1) // BLOCK

    @pl.loop(0, heads)
    def _(h):
        head = g * heads + h
        hit = jnp.zeros((blocks, BAND), jnp.int32)
        listed_block = jnp.zeros((blocks, vert_rows), jnp.int32)
        for n in range(listed):
            hit = jnp.where(target == vertical[head, n], 1, hit)
            listed_block = jnp.where(vplace == n, vertical[head, n], listed_block)
        for n in range(slash.shape[0]):
            hit = jnp.where(offset == slash[n, head], 1, hit)
        seen = (hit == 1) & (offset >= 0) & (offset < REACH) & (target >= 0)
        at = pl.ds(pl.multiple_of(h * blocks, blocks), blocks)
        bias_band[at, :] = jnp.where(seen, 0.0, MASKED)
        bias_vert[at, :] = jnp.where(listed_block <= first + vrow - REACH, 0.0, MASKED)

    own[0].wait()
    own[1].wait()
    for which in range(2):
        kv_pass(which, 0, s).start()

    @pl.loop(1, n_chips)
    def _(d):
        @pl.when(chip >= d)
        def _():
            for which in range(2):
                kv_copy(which, d - 1, s - 2 * d).wait_recv()

                @pl.when(above)
                def _():
                    kv_copy(which, d, s - 2 * d).start()

                kv_pass(which, d, s - 2 * d).start()

    @pl.loop(0, n_chips)
    def _(d):
        @pl.when(chip >= d)
        def _():
            for which in range(2):
                kv_pass(which, d, sibling - 2 * d).wait_recv()

    own[2].wait()

    @pl.loop(0, heads * listed)
    def _(i):
        block = vertical[g * heads + i // listed, i % listed] + 2 * blocks
        kvert[i] = kall[block]
        vvert[i] = vall[block]

    scale = math.log2(math.e) / math.sqrt(HEAD)
    across = (((1,), (1,)), ((), ()))
    wide = REACH * BLOCK

    def chunk_rows(c):
        return pl.ds(pl.multiple_of(c * CHUNK, CHUNK), CHUNK)

    def group_cols(group):
        return pl.ds(pl.multiple_of(group * width, width), width)

    near_groups = (g + 1 - 2 * (g % 2), (g + 2) % 4)
    far = (near_groups[0] + 2) % 4

    def a_copy(c, k):
        part = abuf.at[chunk_rows(c), group_cols(g)]
        return pltpu.make_async_remote_copy(
            src_ref=part, dst_ref=part, send_sem=a_send.at[c, k], recv_sem=a_recv.at[c, k],
            device_id={"heads": near_groups[k]}, device_id_type=MESH,
        )

    def a_arrival(c, k):
        part = abuf.at[chunk_rows(c), group_cols(near_groups[k])]
        return pltpu.make_async_copy(part, part, a_recv.at[c, k])

    def half_rows(c, k):
        return pl.ds(pl.multiple_of(c * CHUNK + k * BLOCK, BLOCK), BLOCK)

    def a_relay(c, k):
        part = abuf.at[half_rows(c, k), group_cols(near_groups[k])]
        return pltpu.make_async_remote_copy(
            src_ref=part, dst_ref=part, send_sem=r_send.at[c, k], recv_sem=r_recv.at[c, k],
            device_id={"heads": near_groups[1 - k]}, device_id_type=MESH,
        )

    def far_arrival(c, k):
        part = abuf.at[half_rows(c, k), group_cols(far)]
        return pltpu.make_async_copy(part, part, r_recv.at[c, k])

    def spread(ref, h, c):
        rows = [
            jnp.broadcast_to(ref[pl.ds(h * blocks + c * per_chunk + a, 1), :], (BLOCK, ref.shape[1]))
            for a in range(per_chunk)
        ]
        return jnp.concatenate(rows, axis=0)

    @pl.loop(0, n_chunks)
    def _(c):
        base = first + c * per_chunk

        @pl.loop(0, heads, unroll=2)
        def _(h):
            col = pl.multiple_of(h * HEAD, HEAD)
            qh = q[chunk_rows(c), pl.ds(col, HEAD)]
            vrows = pl.ds(h * listed, listed)

            def flat(ref, at):
                return ref[at].reshape(at.size * BLOCK, HEAD)

            band = lax.dot_general(qh, flat(kall, pl.ds(base, REACH + per_chunk)), across, preferred_element_type=jnp.float32)
            vert = lax.dot_general(qh, flat(kvert, vrows), across, preferred_element_type=jnp.float32)
            band = band * scale + spread(bias_band, h, c)
            vert = vert * scale + spread(bias_vert, h, c)
            i = lax.broadcasted_iota(jnp.int32, (CHUNK, CHUNK), 0)
            j = lax.broadcasted_iota(jnp.int32, (CHUNK, CHUNK), 1)
            near = jnp.where(j <= i, band[:, wide:], MASKED)
            band = band[:, :wide]
            top = jnp.maximum(
                jnp.maximum(jnp.max(band, axis=1, keepdims=True), jnp.max(vert, axis=1, keepdims=True)),
                jnp.max(near, axis=1, keepdims=True),
            )
            band, vert, near = jnp.exp2(band - top), jnp.exp2(vert - top), jnp.exp2(near - top)
            total = (
                jnp.sum(band, axis=1, keepdims=True)
                + jnp.sum(vert, axis=1, keepdims=True)
                + jnp.sum(near, axis=1, keepdims=True)
            )
            mixed = jnp.dot(band.astype(jnp.bfloat16), flat(vall, pl.ds(base, REACH)), preferred_element_type=jnp.float32)
            mixed += jnp.dot(near.astype(jnp.bfloat16), flat(vall, pl.ds(base + REACH, per_chunk)), preferred_element_type=jnp.float32)
            mixed += jnp.dot(vert.astype(jnp.bfloat16), flat(vvert, vrows), preferred_element_type=jnp.float32)
            abuf[chunk_rows(c), pl.ds(pl.multiple_of(g * width + h * HEAD, HEAD), HEAD)] = (
                mixed / total
            ).astype(jnp.bfloat16)

        for k in range(2):
            a_copy(c, k).start()

    tile = min(cols, 256)

    def project(c):
        for k in range(2):
            far_arrival(c, k).wait()

        @pl.loop(0, cols // tile)
        def _(t):
            at = pl.ds(pl.multiple_of(t * tile, tile), tile)
            out[chunk_rows(c), at] = jnp.dot(
                abuf[chunk_rows(c), :], wfull[:, at], preferred_element_type=jnp.float32
            ).astype(out.dtype)

    @pl.loop(0, n_chunks + 1)
    def _(c):
        @pl.when(c < n_chunks)
        def _():
            for k in range(2):
                a_arrival(c, k).wait()
                a_relay(c, k).start()

        @pl.when(c == 1)
        def _():
            own[3].wait()
            for k in range(1, n_heads):
                w_arrival(k).wait()
                w_pass(k, core).start()
            for k in range(1, n_heads):
                w_pass(k, 1 - core).wait_recv()

        @pl.when(c > 0)
        def _():
            project(c - 1)

    @pl.loop(0, n_chunks)
    def _(c):
        for k in range(2):
            a_copy(c, k).wait_send()
            a_relay(c, k).wait_send()

    for k in range(1, n_heads):
        w_copy(k).wait_send()
        w_pass(k, core).wait_send()

    for which in range(2):
        kv_pass(which, 0, s).wait_send()

    @pl.when(above)
    def _():
        for which in range(2):
            kv_first(which).wait_send()

    @pl.loop(1, n_chips)
    def _(d):
        @pl.when(chip >= d)
        def _():
            for which in range(2):
                kv_pass(which, d, s - 2 * d).wait_send()

                @pl.when(above)
                def _():
                    kv_copy(which, d, s - 2 * d).wait_send()


def local(n_heads, n_seq, queries, keys, values, vertical, slash, out_weight):
    tokens, width = queries.shape
    cols = out_weight.shape[1] // n_heads
    heads = width // HEAD
    blocks = tokens // BLOCK
    n_chips = n_seq // 2
    n_chunks = tokens // CHUNK
    vert_rows = vertical.shape[1] * BLOCK
    bf16, dma = jnp.bfloat16, pltpu.SemaphoreType.DMA
    smem = pl.BlockSpec(memory_space=pltpu.SMEM)
    hbm = pl.BlockSpec(memory_space=pltpu.HBM)
    scores = heads * tokens * (BAND + vert_rows)
    return pl.pallas_call(
        functools.partial(kernel, n_heads, n_seq),
        out_shape=jax.ShapeDtypeStruct((tokens, cols), bf16),
        in_specs=[smem, smem, hbm, hbm, hbm, hbm],
        out_specs=pl.BlockSpec(memory_space=pltpu.VMEM),
        scratch_shapes=[
            pltpu.VMEM((tokens, width), bf16),
            pltpu.VMEM(((n_seq + 2) * blocks, BLOCK, HEAD), bf16),
            pltpu.VMEM(((n_seq + 2) * blocks, BLOCK, HEAD), bf16),
            pltpu.VMEM((heads * vertical.shape[1], BLOCK, HEAD), bf16),
            pltpu.VMEM((heads * vertical.shape[1], BLOCK, HEAD), bf16),
            pltpu.VMEM((n_heads * width, cols), bf16),
            pltpu.VMEM((tokens, n_heads * width), bf16),
            pltpu.VMEM((heads * blocks, BAND), jnp.float32),
            pltpu.VMEM((heads * blocks, vert_rows), jnp.float32),
            dma((4,)),
            dma((2, n_chips)), dma((2, n_chips)), dma((2, n_chips)), dma((2, n_chips)),
            dma((n_heads,)), dma((n_heads,)), dma((n_heads,)), dma((n_heads,)),
            dma((n_chunks, 2)), dma((n_chunks, 2)), dma((n_chunks, 2)), dma((n_chunks, 2)),
        ],
        compiler_params=pltpu.CompilerParams(
            collective_id=0, has_side_effects=True, vmem_limit_bytes=60 * 1024 * 1024
        ),
        cost_estimate=pl.CostEstimate(
            flops=4 * scores * HEAD + 2 * tokens * n_heads * width * cols,
            bytes_accessed=8 * 1024 * 1024,
            transcendentals=scores,
        ),
    )(
        vertical, slash.T, queries,
        keys.reshape(blocks, BLOCK, HEAD), values.reshape(blocks, BLOCK, HEAD), out_weight,
    )


def solution(mesh):
    sizes = dict(mesh.shape)
    return jax.shard_map(
        functools.partial(local, sizes["heads"], sizes["seq"]),
        mesh=mesh,
        in_specs=(P("seq", "heads"), P("seq", "heads"), P("seq", "heads"), P(), P(), P("heads", None)),
        out_specs=P("seq", "heads"),
        check_vma=False,
    )
```
